128 devices in a mesh: head: 4 (over x_lo, core), expert: 32 (over z, y, x_hi).
Axes of the slice: x: 4 (x_hi: 2, x_lo: 2; x = x_hi * 2 + x_lo), y: 4, z: 4, core: 2. Of those that a mesh axis runs over, the one named last changes fastest.
Arguments:
- attn: bfloat16 [4096, 4096], P('expert', 'head'), may hold values from -6 to 6
- o_weight: bfloat16 [4096, 4096], P('head'), may hold values from -0.09375 to 0.09375
- residual: bfloat16 [4096, 4096], P('expert'), may hold values from -6 to 6
- expert_ids: int32 [4096, 8], P('expert'), may hold values from 0 to 31, all different within a row; in each aligned block of 128 rows (0 to 127, 128 to 255, ...) at most 64 rows name the same one
- route_weight: bfloat16 [4096, 8], P('expert'), may hold values from 0.099609375 to 1
- gate_weight: bfloat16 [32, 4096, 1536], P('expert', None, 'head'), may hold values from -0.09375 to 0.09375
- up_weight: bfloat16 [32, 4096, 1536], P('expert', None, 'head'), may hold values from -0.09375 to 0.09375
Outputs:
- gram: float32 [32, 1536, 1536], P('expert', 'head')
The draws below stay inside these ranges and needn't reach their ends.
Inputs may be any that keep to these rules, and one draw needn't show every extreme that they name: `expert_ids`: among the 128 rows of one device no expert is named more than 64 times, a bound that some block reaches; each row names 8 different experts.
All inputs are finite; a program needn't handle non-finite values.
Results may differ from the reference program's by a relative error of at most 0.0065.
Values may be sent and summed in bfloat16 or wider, within the bound.
No kernel may reach another device: no remote copies, remote signals or barrier semaphores. Data moves between devices by JAX's collectives and lax.ppermute only.
A program may use at most 128 MiB of HBM per device.

```python
import math
import jax
import jax.numpy as jnp
import numpy as np
from jax import lax

D = 4096
FF = 1536
HQ = 32
HD = 128
TOP = 8
TOK_DEV = 128
TOKENS = 4096
EXPERTS = 32
CAP = 64
N_EXPERT = 32


def block_scale(stream_key, dims, split, low, top_value):
    loudness, own = 1.0, jax.random.fold_in(stream_key, 6)
    for dim, parts in split:
        steps = jnp.exp(jax.random.uniform(jax.random.fold_in(own, dim), (parts,), jnp.float32, low / len(split), top_value / len(split)))
        loudness = loudness * jnp.repeat(steps, dims[dim] // parts).reshape([-1 if axis == dim else 1 for axis in range(len(dims))])
    return loudness


def routed_block(stream_key, own, number, rows, number_of, top, most, slope):
    ranking = jax.random.permutation(stream_key, number_of)
    packed, usual = load_shares(number_of, rows * top, most, slope, True), load_shares(number_of, rows * top, most, slope, False)
    places = jnp.arange(number_of)

    def named(tallies, turn):
        used = int((tallies > 0).sum())
        fixed = max(1, used // 4)
        moved = fixed + (places - fixed + turn * (used - fixed)) % max(1, number_of - fixed)
        return jnp.zeros((number_of,), jnp.int32).at[ranking[jnp.where(places < fixed, places, moved)]].set(jnp.asarray(tallies, jnp.int32))

    tallies = jnp.where(number % 4 == 0, named(packed, number // 4), named(usual, number - number // 4 - 1))
    mixed = jax.random.permutation(jax.random.fold_in(own, 3), number_of)
    donor, receiver = mixed[0:number_of // 2 * 2:2], mixed[1:number_of // 2 * 2:2]
    margin = jnp.minimum(tallies[donor] - 1, most - tallies[receiver]) // 2
    margin = jnp.where((donor == ranking[0]) | (receiver == ranking[0]) | (tallies[receiver] == 0), 0, jnp.maximum(margin, 0))
    moved = jax.random.randint(jax.random.fold_in(own, 4), (number_of // 2,), 0, 1 << 20) % (margin + 1)
    tallies = tallies.at[donor].add(-moved).at[receiver].add(moved)
    members = jnp.searchsorted(jnp.cumsum(tallies), jnp.arange(rows * top), side="right").astype(jnp.int32)
    table = members.reshape(top, rows).T
    table = table[jax.random.permutation(jax.random.fold_in(own, 1), rows)]
    turn = jax.random.randint(jax.random.fold_in(own, 2), (rows, 1), 0, top)
    return jnp.take_along_axis(table, (jnp.arange(top)[None, :] + turn) % top, axis=1)


def load_shares(number_of, total, most, skew, full):
    weights = [(1 << 20) // math.isqrt(grade ** skew) + 1 for grade in range(1, number_of + 1)]
    largest = most if full else min(most, max(-(-total // number_of), total * weights[0] // sum(weights)))
    least = 1 if total - largest >= number_of - 1 else 0
    given, rest = [largest] + [least] * (number_of - 1), total - largest - least * (number_of - 1)
    while rest > 0:
        movable = [i for i in range(1, number_of) if given[i] < largest] or [i for i in range(1, number_of) if given[i] < most]
        mass, left = sum([weights[i] for i in movable]), rest
        for i in movable:
            addition = min(most - given[i], max(1, left * weights[i] // mass), rest)
            given[i] = given[i] + addition
            rest = rest - addition
    return np.array(given)


def noise(own_key, shape, width, reach, pieces=(), held_as=jnp.bfloat16):
    drawn = width * jax.random.normal(own_key, shape, jnp.float32)
    if pieces:
        drawn = drawn * block_scale(own_key, shape, pieces, -0.22, 0.18)
    return jnp.clip(drawn, -reach, reach).astype(held_as)


def setup_inputs(seed: int = 0) -> dict:
    key_of = jax.random.split(jax.random.key(seed), 8)
    attn = noise(key_of[0], (TOKENS, HQ * HD), 1.0, 6.0, ((0, 32), (1, 4)))
    o_weight = noise(key_of[1], (HQ * HD, D), (HQ * HD) ** -0.5, 0.09375, ((0, 4),))
    residual = noise(key_of[2], (TOKENS, D), 1.0, 6.0, ((0, 32),))
    expert_ids_keys = jax.random.split(jax.random.fold_in(key_of[3], 1), TOKENS // TOK_DEV)
    expert_ids_turns = jax.random.permutation(jax.random.fold_in(key_of[3], 3), TOKENS // TOK_DEV)
    expert_ids = jax.vmap(lambda own, number: routed_block(jax.random.fold_in(key_of[3], 2), own, number, TOK_DEV, EXPERTS, TOP, CAP, 2))(expert_ids_keys, expert_ids_turns).reshape((TOKENS, TOP))
    route_weight = jnp.clip(jnp.exp(math.log(1.0) - 2.306499 * jax.random.uniform(key_of[4], (TOKENS, TOP), jnp.float32) ** block_scale(key_of[4], (TOKENS, TOP), ((0, 32),), -0.2, 0.2)), 0.099609375, 1.0).astype(jnp.bfloat16)
    gate_weight = noise(key_of[5], (EXPERTS, D, FF), D ** -0.5, 0.09375, ((0, 32), (2, 4)))
    up_weight = noise(key_of[6], (EXPERTS, D, FF), D ** -0.5, 0.09375, ((0, 32), (2, 4)))
    return {"attn": attn, "o_weight": o_weight, "residual": residual, "expert_ids": expert_ids, "route_weight": route_weight, "gate_weight": gate_weight, "up_weight": up_weight}


def reference(attn, o_weight, residual, expert_ids, route_weight, gate_weight, up_weight):
    attn_out = jnp.dot(attn, o_weight, preferred_element_type=jnp.float32)
    mixed = residual.astype(jnp.float32) + attn_out
    scale = lax.rsqrt(lax.optimization_barrier(jnp.mean(mixed * mixed, axis=-1)) + 1e-06)
    normed = (mixed * scale[:, None]).astype(jnp.bfloat16)
    limit = N_EXPERT * CAP

    def one_expert(index):
        hits = expert_ids == index
        token_weight = lax.optimization_barrier(jnp.sum(jnp.where(hits, route_weight.astype(jnp.float32), jnp.float32(0.0)), axis=1))
        routed = jnp.any(hits, axis=1)
        order = jnp.argsort(jnp.where(routed, 0, 1).astype(jnp.int32), stable=True)[:limit].astype(jnp.int32)
        chosen = normed[order]
        weights = token_weight[order]
        gate = jnp.dot(chosen, gate_weight[index], preferred_element_type=jnp.float32)
        up = jnp.dot(chosen, up_weight[index], preferred_element_type=jnp.float32)
        keys = (jax.nn.silu(gate) * up).astype(jnp.bfloat16)
        scaled = (keys.astype(jnp.float32) * weights[:, None]).astype(jnp.bfloat16)
        outer = jnp.dot(scaled.T, keys, preferred_element_type=jnp.float32)
        return outer / jnp.sum(weights)
    return lax.map(one_expert, jnp.arange(EXPERTS, dtype=jnp.int32))
```

```python
import jax
import jax.numpy as jnp
from jax import lax
from jax.sharding import PartitionSpec as P

BF16, F32 = jnp.bfloat16, jnp.float32
PEER = F32
AXES = ("head", "expert")
NZ, NY, NX, NC = 4, 4, 4, 2


def moves(place):
    pairs = []
    for x in range(NX):
        for c in range(NC):
            for z in range(NZ):
                for y in range(NY):
                    flat = []
                    for px, pc, pz, py in ((x, c, z, y), place(x, c, z, y)):
                        px, pz, py = px % NX, pz % NZ, py % NY
                        flat.append(((px % 2) * 2 + pc) * 32 + pz * 8 + py * 2 + px // 2)
                    pairs.append(tuple(flat))
    return pairs


CORE = moves(lambda x, c, z, y: (x, 1 - c, z, y))
X_LO = moves(lambda x, c, z, y: (x ^ 1, c, z, y))


def along_x(d):
    return moves(lambda x, c, z, y: (x + d, c, z, y))


def along_first(d):
    return moves(lambda x, c, z, y: (x, c, z + d, y) if c == 0 else (x, c, z, y + d))


def along_last(d):
    return moves(lambda x, c, z, y: (x, c, z, y + d) if c == 0 else (x, c, z + d, y))


def send(value, pairs):
    return lax.ppermute(value, AXES, pairs)


def one_hot(index, size):
    return (index[..., None] == jnp.arange(size, dtype=jnp.int32)).astype(BF16)


def pick(sel, table):
    return jnp.dot(sel, table, preferred_element_type=F32)


def slots_of(weights):
    hit = weights > 0
    tok = jnp.arange(128, dtype=jnp.int32)
    earlier = (tok[:, None] < tok[None, :]).astype(BF16)
    rank = jnp.dot(hit.astype(BF16), earlier, preferred_element_type=F32)
    half = jnp.arange(2, dtype=jnp.int32)[:, None] * 64
    return jnp.where(hit, rank.astype(jnp.int32) + half, -1)


def body(attn, o_weight, residual, expert_ids, route_weight, gate_weight, up_weight):
    head, own = lax.axis_index("head"), lax.axis_index("expert")
    c, x_lo = head % 2, head // 2
    x_hi, y, z = own % 2, (own // 2) % 4, own // 8
    x = x_hi * 2 + x_lo
    rel = jnp.arange(4, dtype=jnp.int32)

    named = expert_ids[None] == jnp.arange(32, dtype=jnp.int32)[:, None, None]
    route = jnp.sum(jnp.where(named, route_weight.astype(F32)[None], 0.0), axis=2).astype(BF16)
    other = send(route, along_x(2))
    line_route = jnp.stack([jnp.where(x_hi == 0, route, other), jnp.where(x_hi == 0, other, route)])
    near = [line_route] + [send(line_route, along_first(-d)) for d in (1, 2, 3)]
    expert_of = jnp.where(
        c == 0, z * 8 + ((y - rel) % 4) * 2 + x_hi, ((z - rel) % 4) * 8 + y * 2 + x_hi
    )
    near = jnp.einsum(
        "je,ahet->jaht", one_hot(expert_of, 32), jnp.stack(near), preferred_element_type=F32
    ).astype(BF16)
    far = jnp.stack([near[0]] + [send(near[j], along_last(-j)) for j in (1, 2, 3)])

    give = lax.dynamic_slice_in_dim(o_weight, (1 - c) * 2048, 2048, axis=1)
    keep = lax.dynamic_slice_in_dim(o_weight, c * 2048, 2048, axis=1)
    give = jnp.dot(attn, give, preferred_element_type=F32).astype(BF16)
    gate_weight, up_weight, give = lax.optimization_barrier((gate_weight, up_weight, give))
    from_core = send(give, CORE).astype(F32)
    keep = jnp.dot(attn, keep, preferred_element_type=F32) + from_core
    give = lax.dynamic_slice_in_dim(keep, (1 - x_lo) * 64, 64, axis=0)
    from_x = send(give.astype(BF16), X_LO).astype(F32)
    res = lax.dynamic_slice(residual, (x_lo * 64, c * 2048), (64, 2048)).astype(F32)
    mixed = res + (lax.dynamic_slice_in_dim(keep, x_lo * 64, 64, axis=0) + from_x)
    squares = jnp.sum(mixed * mixed, axis=1)
    squares = squares + send(squares, CORE)
    x0 = (mixed * lax.rsqrt(squares / 4096 + 1e-06)[:, None]).astype(BF16)

    line0 = jnp.concatenate([x0] + [send(x0, along_x(-d)) for d in (1, 2, 3)], axis=0)
    lines = [line0] + [send(line0, along_first(-d)) for d in (1, 2, 3)]

    def halves(at):
        return [lax.dynamic_slice_in_dim(w[0], at * 2048, 2048, axis=0) for w in (gate_weight, up_weight)]

    w_own = halves(c)
    w_peer = send(jnp.concatenate(halves(1 - c), axis=1), CORE)

    slots = slots_of(near).reshape(16, 256)
    place = jnp.arange(256, dtype=jnp.int32)
    at_x = (x + place // 64) % 4
    token = (at_x // 2) * 128 + (at_x % 2) * 64 + place % 64
    slots = pick((slots + 1).astype(BF16), one_hot(token, 256).T).astype(jnp.int32) - 1
    select = (
        slots.reshape(4, 4, 1, 256) == jnp.arange(128, dtype=jnp.int32)[:, None]
    ).astype(BF16)

    far = far.reshape(4, 4, 1, 256)
    far_slots = slots_of(far.reshape(4, 4, 2, 128)).reshape(4, 4, 1, 256)
    far = far.astype(F32)
    total = jnp.sum(far)
    weights = jnp.sum(
        jnp.where(far_slots == jnp.arange(128, dtype=jnp.int32)[:, None], far, 0.0), axis=3
    )

    rows = [
        jnp.dot(select[:, a].reshape(512, 256), line, preferred_element_type=F32)
        .astype(BF16)
        .reshape(4, 128, 2048)
        for a, line in enumerate(lines)
    ]

    def other_order(value, k):
        blocks = [value[((k - j) % 4) * 128 : ((k - j) % 4) * 128 + 128] for j in range(4)]
        return jnp.concatenate(blocks, axis=0)

    gram = None
    for k in range(4):
        got = [rows[k][0]] + [send(rows[(k - j) % 4][j], along_last(-j)) for j in (1, 2, 3)]
        got = jnp.concatenate(got, axis=0)
        for_peer = jnp.dot(got, w_peer, preferred_element_type=F32).astype(PEER)
        from_peer = send(other_order(for_peer, k), CORE).astype(F32)
        gate = jnp.dot(got, w_own[0], preferred_element_type=F32) + from_peer[:, :384]
        up = jnp.dot(got, w_own[1], preferred_element_type=F32) + from_peer[:, 384:]
        keys = (jax.nn.silu(gate) * up).astype(BF16)
        weight = jnp.concatenate([weights[j, (k - j) % 4] for j in range(4)])
        scaled = (keys.astype(F32) * weight[:, None]).astype(BF16)
        keys_x = send(keys, X_LO)
        keys_c = send(other_order(keys, k), CORE)
        keys_xc = send(other_order(keys_x, k), CORE)
        here = [jnp.where(c == 0, keys, keys_c), jnp.where(c == 0, keys_c, keys)]
        there = [jnp.where(c == 0, keys_x, keys_xc), jnp.where(c == 0, keys_xc, keys_x)]
        columns = [jnp.where(x_lo == 0, a, b) for a, b in zip(here, there)]
        columns += [jnp.where(x_lo == 0, b, a) for a, b in zip(here, there)]
        part = lax.dot_general(
            scaled,
            jnp.concatenate(columns, axis=1),
            (((0,), (0,)), ((), ())),
            preferred_element_type=F32,
        )
        gram = part if gram is None else gram + part
    return (gram / total)[None]


def solution(mesh):
    return jax.shard_map(
        body,
        mesh=mesh,
        in_specs=(
            P("expert", "head"),
            P("head", None),
            P("expert", None),
            P("expert", None),
            P("expert", None),
            P("expert", None, "head"),
            P("expert", None, "head"),
        ),
        out_specs=P("expert", "head", None),
        check_vma=False,
    )
```

```python
import functools

import jax
import jax.numpy as jnp
from jax import lax
from jax.experimental import pallas as pl
from jax.experimental.pallas import tpu as pltpu
from jax.sharding import PartitionSpec as P

BF16, F32 = jnp.bfloat16, jnp.float32
PEER = F32
COST = 1000
WIDE = 2048 + 128
AXES = ("head", "expert")
NZ, NY, NX, NC = 4, 4, 4, 2


def moves(place):
    pairs = []
    for x in range(NX):
        for c in range(NC):
            for z in range(NZ):
                for y in range(NY):
                    flat = []
                    for px, pc, pz, py in ((x, c, z, y), place(x, c, z, y)):
                        px, pz, py = px % NX, pz % NZ, py % NY
                        flat.append(((px % 2) * 2 + pc) * 32 + pz * 8 + py * 2 + px // 2)
                    pairs.append(tuple(flat))
    return pairs


CORE = moves(lambda x, c, z, y: (x, 1 - c, z, y))
X_LO = moves(lambda x, c, z, y: (x ^ 1, c, z, y))


def along_x(d):
    return moves(lambda x, c, z, y: (x + d, c, z, y))


def along_first(d):
    return moves(lambda x, c, z, y: (x, c, z + d, y) if c == 0 else (x, c, z, y + d))


def along_last(d):
    return moves(lambda x, c, z, y: (x, c, z, y + d) if c == 0 else (x, c, z + d, y))


def send(value, pairs):
    return lax.ppermute(value, AXES, pairs)


def together(*values):
    return lax.optimization_barrier(values)


def first_sums(attn, o_weight, c, x_lo):
    give = lax.dynamic_slice_in_dim(o_weight, (1 - c) * 2048, 2048, axis=1)
    give = jnp.dot(attn, give, preferred_element_type=F32).astype(BF16)
    from_core = send(give, CORE).astype(F32)
    keep = lax.dynamic_slice_in_dim(o_weight, c * 2048, 2048, axis=1)
    keep = jnp.dot(attn, keep, preferred_element_type=F32) + from_core
    return keep, lax.dynamic_slice_in_dim(keep, (1 - x_lo) * 64, 64, axis=0).astype(BF16)


def lane_of(index):
    return (lax.broadcasted_iota(jnp.int32, (128, 128), 0) == index).astype(F32).astype(BF16)


def products(k, own, row0, row1, row2, row3, w_peer, w_own, for_peer, for_own, weight, rows):
    for j, block in enumerate((row0, row1, row2, row3)):
        rows[j * 128 : (j + 1) * 128, :] = block[...]
    for h in range(2):
        here = slice(h * 384, (h + 1) * 384)
        made = jnp.dot(rows[:, :2048], w_peer[:, here], preferred_element_type=F32).astype(PEER)
        for j in range(4):
            i = (k - j) % 4
            for_peer[j * 128 : (j + 1) * 128, here] = made[i * 128 : (i + 1) * 128]
    for h in range(2):
        here = slice(h * 384, (h + 1) * 384)
        for_own[:, here] = jnp.dot(rows[:, :2048], w_own[:, here], preferred_element_type=F32)
    weight[...] = jnp.dot(rows[:, 2048:], lane_of(own[0]), preferred_element_type=F32)


def chunk_products(k, own, blocks, w_peer, w_own):
    vmem = pl.BlockSpec(memory_space=pltpu.VMEM)
    return pl.pallas_call(
        functools.partial(products, k),
        out_shape=(
            jax.ShapeDtypeStruct((512, 768), PEER),
            jax.ShapeDtypeStruct((512, 768), F32),
            jax.ShapeDtypeStruct((512, 128), F32),
        ),
        in_specs=[pl.BlockSpec(memory_space=pltpu.SMEM)] + [vmem] * 6,
        out_specs=(vmem,) * 3,
        scratch_shapes=[pltpu.VMEM((512, WIDE), BF16)],
        compiler_params=pltpu.CompilerParams(vmem_limit_bytes=16 * 2**20),
        cost_estimate=pl.CostEstimate(flops=COST, bytes_accessed=COST, transcendentals=0),
    )(own, *blocks, w_peer, w_own)


def pick_rows(where, line0, line1, line2, line3, *out):
    place = lax.broadcasted_iota(jnp.int32, (256, 256), 0) + where[4] * 64
    other = lax.broadcasted_iota(jnp.int32, (256, 256), 1) + where[4] * 64
    earlier = jnp.where((other & 255) < (place & 255), 1.0, 0.0).astype(BF16)
    lane = lax.broadcasted_iota(jnp.int32, (256, 128), 1).astype(F32)
    for a, line in enumerate((line0, line1, line2, line3)):
        hit = line[:, 2048:].astype(F32) > 0
        rank = jnp.dot(
            earlier, jnp.where(hit, 1.0, 0.0).astype(BF16), preferred_element_type=F32
        )
        rank = jnp.where(hit, rank, 255.0).astype(BF16)
        select = []
        for j in range(4):
            slot = jnp.dot(rank, lane_of(where[j]), preferred_element_type=F32)
            select.append(jnp.where(slot == lane, 1.0, 0.0).astype(BF16))
        made = lax.dot_general(
            jnp.concatenate(select, axis=1),
            line[...],
            (((0,), (0,)), ((), ())),
            preferred_element_type=F32,
        ).astype(BF16)
        for j in range(4):
            out[(a + j) % 4 * 4 + j][...] = made[j * 128 : (j + 1) * 128]


def picked_rows(where, lines):
    vmem = pl.BlockSpec(memory_space=pltpu.VMEM)
    return pl.pallas_call(
        pick_rows,
        out_shape=(jax.ShapeDtypeStruct((128, WIDE), BF16),) * 16,
        in_specs=[pl.BlockSpec(memory_space=pltpu.SMEM)] + [vmem] * 4,
        out_specs=(vmem,) * 16,
        compiler_params=pltpu.CompilerParams(vmem_limit_bytes=20 * 2**20),
        cost_estimate=pl.CostEstimate(flops=COST, bytes_accessed=COST, transcendentals=0),
    )(where, *lines)


def finish_keys(for_own, from_peer, weight, keys, scaled, total):
    gate = for_own[:, :384] + from_peer[:, :384].astype(F32)
    up = for_own[:, 384:] + from_peer[:, 384:].astype(F32)
    made = (gate / (1.0 + jnp.exp(-gate)) * up).astype(BF16)
    keys[...] = made
    scaled[...] = (made.astype(F32) * weight[:, :1]).astype(BF16)
    total[...] = jnp.sum(weight[...], axis=0, keepdims=True)


def chunk_keys(for_own, from_peer, weight):
    vmem = pl.BlockSpec(memory_space=pltpu.VMEM)
    return pl.pallas_call(
        finish_keys,
        out_shape=(
            jax.ShapeDtypeStruct((512, 384), BF16),
            jax.ShapeDtypeStruct((512, 384), BF16),
            jax.ShapeDtypeStruct((1, 128), F32),
        ),
        in_specs=[vmem] * 3,
        out_specs=(vmem,) * 3,
        compiler_params=pltpu.CompilerParams(vmem_limit_bytes=12 * 2**20),
        cost_estimate=pl.CostEstimate(flops=COST, bytes_accessed=COST, transcendentals=0),
    )(for_own, from_peer, weight)


def body(attn, o_weight, residual, expert_ids, route_weight, gate_weight, up_weight):
    head, own = lax.axis_index("head"), lax.axis_index("expert")
    c, x_lo = head % 2, head // 2
    x_hi, y, z = own % 2, (own // 2) % 4, own // 8
    rel = jnp.arange(4, dtype=jnp.int32)

    keep, give = first_sums(attn, o_weight, c, x_lo)
    from_x = send(give, X_LO).astype(F32)
    res = lax.dynamic_slice(residual, (x_lo * 64, c * 2048), (64, 2048)).astype(F32)
    mixed = res + (lax.dynamic_slice_in_dim(keep, x_lo * 64, 64, axis=0) + from_x)
    squares = jnp.sum(mixed * mixed, axis=1)
    squares = squares + send(squares, CORE)
    normed = (mixed * lax.rsqrt(squares / 4096 + 1e-06)[:, None]).astype(BF16)

    ids = lax.dynamic_slice_in_dim(expert_ids, x_lo * 64, 64, axis=0)
    chosen = lax.dynamic_slice_in_dim(route_weight, x_lo * 64, 64, axis=0).astype(F32)
    named = ids[:, :, None] == jnp.arange(128, dtype=jnp.int32)
    route = jnp.sum(jnp.where(named, chosen[:, :, None], 0.0), axis=1).astype(BF16)
    x0 = jnp.concatenate([normed, route], axis=1)
    gate_weight, up_weight, x0 = together(gate_weight, up_weight, x0)

    line0 = jnp.concatenate([x0] + [send(x0, along_x(-d)) for d in (1, 2, 3)], axis=0)
    lines = [line0] + [send(line0, along_first(-d)) for d in (1, 2, 3)]

    def halves(at):
        return jnp.concatenate(
            [lax.dynamic_slice_in_dim(w[0], at * 2048, 2048, axis=0) for w in (gate_weight, up_weight)],
            axis=1,
        )

    w_own = halves(c)
    w_peer = send(halves(1 - c), CORE)

    experts = jnp.where(
        c == 0, z * 8 + ((y - rel) % 4) * 2 + x_hi, ((z - rel) % 4) * 8 + y * 2 + x_hi
    )
    where = jnp.concatenate([experts, (x_hi * 2 + x_lo)[None]])
    picked = picked_rows(where, lines)

    def other_order(value, k):
        blocks = [value[((k - j) % 4) * 128 : ((k - j) % 4) * 128 + 128] for j in range(4)]
        return jnp.concatenate(blocks, axis=0)

    own = own[None]
    got = []
    for k in range(4):
        got.append([send(picked[4 * k + j], along_last(-j)) for j in (1, 2, 3)])
    for_peer, for_own, weight = [None] * 4, [None] * 4, [None] * 4
    keys, scaled, total = [None] * 4, [None] * 4, [None] * 4

    def multiply(k):
        blocks = [picked[4 * k]] + list(got[k])
        for_peer[k], for_own[k], weight[k] = chunk_products(k, own, blocks, w_peer, w_own)

    def finish(k):
        from_peer = send(for_peer[k], CORE)
        keys[k], scaled[k], total[k] = chunk_keys(for_own[k], from_peer, weight[k])

    multiply(0)
    for_peer[0], *got[1] = together(for_peer[0], *got[1])
    finish(0)
    multiply(1)
    crossed = [send(keys[0], X_LO)]
    crossed[0], for_peer[1], *got[2] = together(crossed[0], for_peer[1], *got[2])
    finish(1)
    multiply(2)
    crossed.append(send(keys[1], X_LO))
    crossed[1], for_peer[2], *got[3] = together(crossed[1], for_peer[2], *got[3])
    finish(2)
    multiply(3)
    crossed.append(send(keys[2], X_LO))
    finish(3)
    crossed.append(send(keys[3], X_LO))

    gram = None
    for k in range(4):
        both = jnp.concatenate([other_order(keys[k], k), other_order(crossed[k], k)], axis=1)
        keys_c, keys_xc = jnp.split(send(both, CORE), 2, axis=1)
        here = [jnp.where(c == 0, keys[k], keys_c), jnp.where(c == 0, keys_c, keys[k])]
        there = [jnp.where(c == 0, crossed[k], keys_xc), jnp.where(c == 0, keys_xc, crossed[k])]
        columns = [jnp.where(x_lo == 0, a, b) for a, b in zip(here, there)]
        columns += [jnp.where(x_lo == 0, b, a) for a, b in zip(here, there)]
        part = lax.dot_general(
            scaled[k],
            jnp.concatenate(columns, axis=1),
            (((0,), (0,)), ((), ())),
            preferred_element_type=F32,
        )
        gram = part if gram is None else gram + part
    total = sum(total)[0, 0]
    return (gram / total)[None]


def solution(mesh):
    return jax.shard_map(
        body,
        mesh=mesh,
        in_specs=(
            P("expert", "head"),
            P("head", None),
            P("expert", None),
            P("expert", None),
            P("expert", None),
            P("expert", None, "head"),
            P("expert", None, "head"),
        ),
        out_specs=P("expert", "head", None),
        check_vma=False,
    )
```

```python
import functools

import jax
import jax.numpy as jnp
from jax import lax
from jax.experimental import pallas as pl
from jax.experimental.pallas import tpu as pltpu
from jax.sharding import PartitionSpec as P

BF16, F32 = jnp.bfloat16, jnp.float32
PEER = F32
COST = 1000
ORDER = (2, 1, 3, 0)
WIDE = 2048 + 128
AXES = ("head", "expert")
NZ, NY, NX, NC = 4, 4, 4, 2


def moves(place):
    pairs = []
    for x in range(NX):
        for c in range(NC):
            for z in range(NZ):
                for y in range(NY):
                    flat = []
                    for px, pc, pz, py in ((x, c, z, y), place(x, c, z, y)):
                        px, pz, py = px % NX, pz % NZ, py % NY
                        flat.append(((px % 2) * 2 + pc) * 32 + pz * 8 + py * 2 + px // 2)
                    pairs.append(tuple(flat))
    return pairs


CORE = moves(lambda x, c, z, y: (x, 1 - c, z, y))
X_LO = moves(lambda x, c, z, y: (x ^ 1, c, z, y))


def along_x(d):
    return moves(lambda x, c, z, y: (x + d, c, z, y))


def along_first(d):
    return moves(lambda x, c, z, y: (x, c, z + d, y) if c == 0 else (x, c, z, y + d))


def along_last(d):
    return moves(lambda x, c, z, y: (x, c, z, y + d) if c == 0 else (x, c, z + d, y))


def send(value, pairs):
    return lax.ppermute(value, AXES, pairs)


def together(*values):
    return lax.optimization_barrier(values)


def first_sums(attn, o_weight, c, x_lo):
    give = lax.dynamic_slice_in_dim(o_weight, (1 - c) * 2048, 2048, axis=1)
    give = jnp.dot(attn, give, preferred_element_type=F32).astype(BF16)
    from_core = send(give, CORE).astype(F32)
    keep = lax.dynamic_slice_in_dim(o_weight, c * 2048, 2048, axis=1)
    keep = jnp.dot(attn, keep, preferred_element_type=F32) + from_core
    return keep, lax.dynamic_slice_in_dim(keep, (1 - x_lo) * 64, 64, axis=0).astype(BF16)


def lane_of(index):
    return (lax.broadcasted_iota(jnp.int32, (128, 128), 0) == index).astype(F32).astype(BF16)


def products(k, own, row0, row1, row2, row3, w_peer, w_own, for_peer, for_own, weight, rows):
    for j, block in enumerate((row0, row1, row2, row3)):
        rows[j * 128 : (j + 1) * 128, :] = block[...]
    for h in range(2):
        here = slice(h * 384, (h + 1) * 384)
        made = jnp.dot(rows[:, :2048], w_peer[:, here], preferred_element_type=F32).astype(PEER)
        for j in range(4):
            i = (k - j) % 4
            for_peer[j * 128 : (j + 1) * 128, here] = made[i * 128 : (i + 1) * 128]
    for h in range(2):
        here = slice(h * 384, (h + 1) * 384)
        for_own[:, here] = jnp.dot(rows[:, :2048], w_own[:, here], preferred_element_type=F32)
    weight[...] = jnp.dot(rows[:, 2048:], lane_of(own[0]), preferred_element_type=F32)


def chunk_products(k, own, blocks, w_peer, w_own):
    vmem = pl.BlockSpec(memory_space=pltpu.VMEM)
    return pl.pallas_call(
        functools.partial(products, k),
        out_shape=(
            jax.ShapeDtypeStruct((512, 768), PEER),
            jax.ShapeDtypeStruct((512, 768), F32),
            jax.ShapeDtypeStruct((512, 128), F32),
        ),
        in_specs=[pl.BlockSpec(memory_space=pltpu.SMEM)] + [vmem] * 6,
        out_specs=(vmem,) * 3,
        scratch_shapes=[pltpu.VMEM((512, WIDE), BF16)],
        compiler_params=pltpu.CompilerParams(vmem_limit_bytes=16 * 2**20),
        cost_estimate=pl.CostEstimate(flops=COST, bytes_accessed=COST, transcendentals=0),
    )(own, *blocks, w_peer, w_own)


def pick_rows(where, line, *out):
    place = lax.broadcasted_iota(jnp.int32, (256, 256), 0) + where[4] * 64
    other = lax.broadcasted_iota(jnp.int32, (256, 256), 1) + where[4] * 64
    earlier = jnp.where((other & 255) < (place & 255), 1.0, 0.0).astype(BF16)
    lane = lax.broadcasted_iota(jnp.int32, (256, 128), 1).astype(F32)
    hit = line[:, 2048:].astype(F32) > 0
    rank = jnp.dot(earlier, jnp.where(hit, 1.0, 0.0).astype(BF16), preferred_element_type=F32)
    rank = jnp.where(hit, rank, 255.0).astype(BF16)
    select = []
    for j in range(4):
        slot = jnp.dot(rank, lane_of(where[j]), preferred_element_type=F32)
        select.append(jnp.where(slot == lane, 1.0, 0.0).astype(BF16))
    made = lax.dot_general(
        jnp.concatenate(select, axis=1),
        line[...],
        (((0,), (0,)), ((), ())),
        preferred_element_type=F32,
    ).astype(BF16)
    for j in range(4):
        out[j][...] = made[j * 128 : (j + 1) * 128]


def picked_rows(where, line):
    vmem = pl.BlockSpec(memory_space=pltpu.VMEM)
    return pl.pallas_call(
        pick_rows,
        out_shape=(jax.ShapeDtypeStruct((128, WIDE), BF16),) * 4,
        in_specs=[pl.BlockSpec(memory_space=pltpu.SMEM), vmem],
        out_specs=(vmem,) * 4,
        compiler_params=pltpu.CompilerParams(vmem_limit_bytes=20 * 2**20),
        cost_estimate=pl.CostEstimate(flops=COST, bytes_accessed=COST, transcendentals=0),
    )(where, line)


def finish_keys(for_own, from_peer, weight, keys, scaled, total):
    gate = for_own[:, :384] + from_peer[:, :384].astype(F32)
    up = for_own[:, 384:] + from_peer[:, 384:].astype(F32)
    made = (gate / (1.0 + jnp.exp(-gate)) * up).astype(BF16)
    keys[...] = made
    scaled[...] = (made.astype(F32) * weight[:, :1]).astype(BF16)
    total[...] = jnp.sum(weight[...], axis=0, keepdims=True)


def chunk_keys(for_own, from_peer, weight):
    vmem = pl.BlockSpec(memory_space=pltpu.VMEM)
    return pl.pallas_call(
        finish_keys,
        out_shape=(
            jax.ShapeDtypeStruct((512, 384), BF16),
            jax.ShapeDtypeStruct((512, 384), BF16),
            jax.ShapeDtypeStruct((1, 128), F32),
        ),
        in_specs=[vmem] * 3,
        out_specs=(vmem,) * 3,
        compiler_params=pltpu.CompilerParams(vmem_limit_bytes=12 * 2**20),
        cost_estimate=pl.CostEstimate(flops=COST, bytes_accessed=COST, transcendentals=0),
    )(for_own, from_peer, weight)


def add_gram(first, last, head, scaled, keys, keys_c, keys_x, keys_xc, total, *refs):
    gram = refs[-1]
    odd, far = head[0] % 2 == 1, head[0] // 2 == 1
    own, peer, own_x, peer_x = keys[...], keys_c[...], keys_x[...], keys_xc[...]
    here = jnp.where(odd, peer, own), jnp.where(odd, own, peer)
    there = jnp.where(odd, peer_x, own_x), jnp.where(odd, own_x, peer_x)
    for n, (a, b) in enumerate(zip(here + there, there + here)):
        at = slice(n * 384, (n + 1) * 384)
        part = lax.dot_general(
            scaled[...],
            jnp.where(far, b, a),
            (((0,), (0,)), ((), ())),
            preferred_element_type=F32,
        )
        if not first:
            part = part + refs[0][:, at]
        if last:
            part = part / total[0:1, 0:1]
        gram[:, at] = part


def chunk_gram(first, last, head, scaled, columns, total, *gram):
    vmem = pl.BlockSpec(memory_space=pltpu.VMEM)
    return pl.pallas_call(
        functools.partial(add_gram, first, last),
        out_shape=jax.ShapeDtypeStruct((384, 1536), F32),
        in_specs=[pl.BlockSpec(memory_space=pltpu.SMEM)] + [vmem] * (6 + len(gram)),
        out_specs=vmem,
        compiler_params=pltpu.CompilerParams(vmem_limit_bytes=16 * 2**20),
        cost_estimate=pl.CostEstimate(flops=COST, bytes_accessed=COST, transcendentals=0),
    )(head, scaled, *columns, total, *gram)


def body(attn, o_weight, residual, expert_ids, route_weight, gate_weight, up_weight):
    head, own = lax.axis_index("head"), lax.axis_index("expert")
    c, x_lo = head % 2, head // 2
    x_hi, y, z = own % 2, (own // 2) % 4, own // 8
    rel = jnp.arange(4, dtype=jnp.int32)

    keep, give = first_sums(attn, o_weight, c, x_lo)
    from_x = send(give, X_LO).astype(F32)
    res = lax.dynamic_slice(residual, (x_lo * 64, c * 2048), (64, 2048)).astype(F32)
    mixed = res + (lax.dynamic_slice_in_dim(keep, x_lo * 64, 64, axis=0) + from_x)
    squares = jnp.sum(mixed * mixed, axis=1)
    squares = squares + send(squares, CORE)
    normed = (mixed * lax.rsqrt(squares / 4096 + 1e-06)[:, None]).astype(BF16)

    ids = lax.dynamic_slice_in_dim(expert_ids, x_lo * 64, 64, axis=0)
    chosen = lax.dynamic_slice_in_dim(route_weight, x_lo * 64, 64, axis=0).astype(F32)
    named = ids[:, :, None] == jnp.arange(128, dtype=jnp.int32)
    route = jnp.sum(jnp.where(named, chosen[:, :, None], 0.0), axis=1).astype(BF16)
    x0 = jnp.concatenate([normed, route], axis=1)
    gate_weight, up_weight, x0 = together(gate_weight, up_weight, x0)

    line0 = jnp.concatenate([x0] + [send(x0, along_x(-d)) for d in (1, 2, 3)], axis=0)
    line1, line3 = send(line0, along_first(-1)), send(line0, along_first(1))
    line2 = jnp.concatenate(
        [send(line1[:128], along_first(-1)), send(line3[128:], along_first(1))], axis=0
    )
    lines = [line0, line1, line2, line3]

    def halves(at):
        return jnp.concatenate(
            [lax.dynamic_slice_in_dim(w[0], at * 2048, 2048, axis=0) for w in (gate_weight, up_weight)],
            axis=1,
        )

    w_own = halves(c)
    w_peer = send(halves(1 - c), CORE)

    experts = jnp.where(
        c == 0, z * 8 + ((y - rel) % 4) * 2 + x_hi, ((z - rel) % 4) * 8 + y * 2 + x_hi
    )
    where = jnp.concatenate([experts, (x_hi * 2 + x_lo)[None]])
    picked = [picked_rows(where, line) for line in lines]

    def other_order(value, k):
        blocks = [value[((k - j) % 4) * 128 : ((k - j) % 4) * 128 + 128] for j in range(4)]
        return jnp.concatenate(blocks, axis=0)

    own = own[None]
    got = []
    for k in range(4):
        got.append([send(picked[(k - j) % 4][j], along_last(-j)) for j in (1, 2, 3)])
    for_peer, for_own, weight = [None] * 4, [None] * 4, [None] * 4
    keys, scaled, total = [None] * 4, [None] * 4, [None] * 4

    def multiply(k):
        blocks = [picked[k][0]] + list(got[k])
        for_peer[k], for_own[k], weight[k] = chunk_products(k, own, blocks, w_peer, w_own)

    def finish(k):
        from_peer = send(for_peer[k], CORE)
        keys[k], scaled[k], total[k] = chunk_keys(for_own[k], from_peer, weight[k])

    k0, k1, k2, k3 = ORDER
    crossed = [None] * 4
    multiply(k0)
    for_peer[k0], *got[k1] = together(for_peer[k0], *got[k1])
    finish(k0)
    multiply(k1)
    crossed[k0] = send(keys[k0], X_LO)
    crossed[k0], for_peer[k1], *got[k2] = together(crossed[k0], for_peer[k1], *got[k2])
    finish(k1)
    multiply(k2)
    crossed[k1] = send(keys[k1], X_LO)
    crossed[k1], for_peer[k2], *got[k3] = together(crossed[k1], for_peer[k2], *got[k3])
    finish(k2)
    multiply(k3)
    crossed[k2] = send(keys[k2], X_LO)
    finish(k3)
    crossed[k3] = send(keys[k3], X_LO)

    gram, total = (), sum(total)
    for i, k in enumerate(ORDER):
        keys_c = send(other_order(keys[k], k), CORE)
        keys_xc = send(other_order(crossed[k], k), CORE)
        columns = keys[k], keys_c, crossed[k], keys_xc
        gram = (chunk_gram(i == 0, i == 3, head[None], scaled[k], columns, total, *gram),)
    return gram[0][None]


def solution(mesh):
    return jax.shard_map(
        body,
        mesh=mesh,
        in_specs=(
            P("expert", "head"),
            P("head", None),
            P("expert", None),
            P("expert", None),
            P("expert", None),
            P("expert", None, "head"),
            P("expert", None, "head"),
        ),
        out_specs=P("expert", "head", None),
        check_vma=False,
    )
```
